32 devices in a mesh: groups: 2 (over x), blk: 8 (over z, y), atoms: 2 (over core).
Axes of the slice: x: 2, y: 2, z: 4, core: 2. Of those that a mesh axis runs over, the one named last changes fastest.
Arguments:
- density: bfloat16 [384, 1024], P('groups', 'blk'), parts along dimension 0, may hold values from -6 to 6
- three_centre: bfloat16 [16, 2, 4, 128, 2048], P(('groups', 'blk'), 'atoms'), parts along dimension 0, may hold values from -0.0078125 to 0.0078125
- pattern: int32 [16, 2, 4], P(('groups', 'blk'), 'atoms'), parts along dimension 0, may hold values from 0 to 7, all different within a row
- domain: int32 [16, 2, 2], P(('groups', 'blk')), parts along dimension 0, may hold values from 0 to 1
- owner: int32 [16, 2], P(('groups', 'blk')), parts along dimension 0, may hold values from 0 to 1, each once within a row
- metric: bfloat16 [16, 2, 1024, 1024], P(('groups', 'blk'), 'atoms'), parts along dimension 0, may hold values from -1 to 3, as said below
Outputs:
- exchange: float32 [16, 2, 192, 192], P(('groups', 'blk'), 'atoms'), parts along dimension 0
The draws below stay inside these ranges and needn't reach their ends.
There are 2 independent parts, one for each index of `groups`. The reference program is written for one: setup_inputs(seed, part) draws one part's arguments, and reference() takes and returns one part's arrays. A program takes and returns all parts, laid end to end along the dimension named above; each array names one. Nothing has to cross between parts.
Inputs may be any that keep to these rules, and one draw needn't show every extreme that they name: `pattern`: each device's entries are different tiles. `owner`: each row is an order of the atom groups. `metric`: each matrix is symmetric with a positive diagonal.
All inputs are finite; a program needn't handle non-finite values.
Results may differ from the reference program's by a relative error of at most 0.0013.
Values may be sent and summed in bfloat16 or wider, within the bound.
No kernel may reach another device: no remote copies, remote signals or barrier semaphores. Data moves between devices by JAX's collectives and lax.ppermute only.
A program may use at most 64 MiB of HBM per device.

```python
import math
import jax
import jax.numpy as jnp
from jax import lax

NOCC = 192
AUX = 1024
TILE = 128
SEGS = 2
NNZ = 4
ROWS = 2048
NBAS = 1024
N_BLK = 8
N_ATOMS = 2


def draw_metric(key, part):
    first, second = jax.random.split(key)
    shape = (N_BLK, N_ATOMS, AUX, AUX)
    diagonal = jnp.exp(jax.random.uniform(first, (N_BLK, N_ATOMS, AUX), jnp.float32, math.log(0.5), math.log(2.0)))
    raw = jax.random.normal(second, shape, jnp.float32) * (0.3 / math.sqrt(AUX))
    spread = (raw + jnp.swapaxes(raw, -1, -2)) * (1.0 / math.sqrt(2.0))
    identity = jnp.eye(AUX, dtype=jnp.float32)
    return (spread * (1.0 - identity) + diagonal[..., None] * identity).astype(jnp.bfloat16)


def plant(array, rng, smallest, largest):
    shape = array.shape
    index_at = [jax.random.randint(jax.random.fold_in(rng, axis), (), 0, shape[axis]) for axis in range(len(shape))]
    array = array.at[tuple(index_at)].set(smallest)
    longest = shape.index(max(shape))
    index_at[longest] = (index_at[longest] + 1) % shape[longest]
    return array.at[tuple(index_at)].set(largest)


def block_scale(key, extent, cuts, low, high):
    def one(dim, shards_of):
        steps = jax.random.uniform(jax.random.fold_in(jax.random.fold_in(key, 6), dim), (shards_of,), jnp.float32, low / len(cuts), high / len(cuts))
        return jnp.repeat(jnp.exp(steps), extent[dim] // shards_of).reshape((-1,) + (1,) * (len(extent) - dim - 1))

    loudness = one(*cuts[0])
    for cut in cuts[1:]:
        loudness = loudness * one(*cut)
    return loudness


def distinct(own_key, rows, number_of, top, lift):
    ranking = jax.random.permutation(jax.random.fold_in(own_key, 1), number_of)
    pull = ranking
    for power in range(3):
        pull = pull * pull // number_of
    pull = pull * lift // number_of
    chance = jax.random.randint(jax.random.fold_in(own_key, 2), (rows, number_of), 0, 4096) + pull
    sure = jax.random.permutation(jax.random.fold_in(own_key, 3), rows)[jnp.arange(number_of) % rows]
    chance = jnp.where(jnp.arange(rows)[:, None] == sure[None, :], 1 << 14, chance)
    merit = chance * number_of + jnp.arange(number_of)
    return lax.top_k(merit.astype(jnp.int32), top)[1].astype(jnp.int32)


def centred(own_key, shape, deviation, limit, shards=(), held_as=jnp.bfloat16):
    drawn = jax.random.normal(own_key, shape, jnp.float32) * deviation
    if len(shards) > 0:
        drawn = block_scale(own_key, shape, shards, -0.22, 0.18) * drawn
    return jnp.clip(drawn, min=-limit, max=limit).astype(held_as)


def setup_inputs(seed: int = 0, part: int = 0) -> dict:
    seeds = jax.random.split(jax.random.key(seed), 7)
    part_splits = jax.random.split(jax.random.fold_in(seeds[6], part), 7)
    return {
        "density": centred(part_splits[0], (NOCC, NBAS), 1.0, 6.0, ((1, 8),)),
        "three_centre": centred(part_splits[1], (N_BLK, N_ATOMS, NNZ, TILE, ROWS), (NNZ * TILE * AUX) ** -0.5, 0.0078125, ((0, 8), (1, 2))),
        "pattern": distinct(part_splits[2], N_BLK * N_ATOMS, N_BLK, NNZ, 0).reshape((N_BLK, N_ATOMS, NNZ)),
        "domain": plant(jax.random.randint(part_splits[3], (N_BLK, N_ATOMS, SEGS), 0, N_ATOMS), jax.random.fold_in(part_splits[3], 1), 0, N_ATOMS - 1).astype(jnp.int32),
        "owner": jax.vmap(lambda own: jax.random.permutation(own, N_ATOMS))(jax.random.split(part_splits[4], N_BLK)).reshape((N_BLK, N_ATOMS)).astype(jnp.int32),
        "metric": draw_metric(jax.random.fold_in(jax.random.fold_in(seeds[6], part), 71), part),
    }


def reference(density, three_centre, pattern, domain, owner, metric):
    tiles = density.reshape(NOCC, N_BLK, TILE).transpose(1, 0, 2)

    def per_block(inputs):
        centre, chosen, domains, owners, metrics = inputs
        picked = tiles[chosen]
        halves = jnp.einsum("aknt,aktr->anr", picked.astype(jnp.float32), centre.astype(jnp.float32), precision=lax.Precision.HIGHEST)
        halves = halves.astype(jnp.bfloat16)
        segments = halves.reshape(N_ATOMS, NOCC, SEGS, AUX).transpose(0, 2, 1, 3).reshape(N_ATOMS * SEGS, NOCC, AUX)
        segments = segments.astype(jnp.float32)
        targets = owners[domains].reshape(N_ATOMS * SEGS).astype(jnp.int32)
        fitted = jnp.einsum("snq,aqp->asnp", segments, metrics.astype(jnp.float32), precision=lax.Precision.HIGHEST)
        fitted = fitted.astype(jnp.bfloat16).astype(jnp.float32)
        products = jnp.einsum("asnp,smp->asnm", fitted, segments, precision=lax.Precision.HIGHEST)
        weights = (targets[None, :] == jnp.arange(N_ATOMS, dtype=jnp.int32)[:, None]).astype(jnp.float32)
        return jnp.einsum("as,asnm->anm", weights, products, precision=lax.Precision.HIGHEST)

    return lax.map(per_block, (three_centre, pattern, domain, owner, metric))
```

```python
import functools
import jax
import jax.numpy as jnp
from jax import lax
from jax.experimental import pallas as pl
from jax.experimental.pallas import tpu as pltpu
from jax.sharding import PartitionSpec as P

AXES = ("blk", "atoms")


def between_blocks(block, count, even, odd):
    pairs = []
    for b in range(count):
        pairs.append((2 * b, 2 * (b ^ even)))
        pairs.append((2 * b + 1, 2 * (b ^ odd) + 1))
    return lax.ppermute(block, AXES, pairs)


def swap_cores(block):
    return lax.ppermute(block, "atoms", [(0, 1), (1, 0)])


def far(array):
    return pltpu.with_memory_space_constraint(array, pltpu.HBM)


def routes(count):
    return [(k, k - 1) for k in range(count - 1, 2, -2)] + [(1, 1)]


def exchange_kernel(plan, count, *refs):
    indices_hbm = refs[:4]
    tiles = refs[4 : 4 + count]
    centre, centre_other, metric, out = refs[4 + count : 8 + count]
    table, dens, rows, matrix, sem = refs[8 + count : 13 + count]
    indices = refs[13 + count : 17 + count]
    index_sem = refs[17 + count]
    pattern, pattern_other, domain, owner = indices
    block = lax.axis_index("blk")
    core = lax.axis_index("atoms")
    segs = domain.shape[2]
    slots, width = centre.shape[2], centre.shape[3]
    aux = metric.shape[2]

    def load(source, seg):
        hbm = centre if source == 0 else centre_other
        return pltpu.make_async_copy(
            hbm.at[0, 0, :, :, pl.ds(seg * aux, aux)], rows.at[source, seg], sem.at[source * segs + seg]
        )

    index_loads = [
        pltpu.make_async_copy(far, near, index_sem.at[i]) for i, (far, near) in enumerate(zip(indices_hbm, indices))
    ]
    own_tile = pltpu.make_async_copy(tiles[0], table.at[block], index_sem.at[4])
    for copy in index_loads + [own_tile]:
        copy.start()
    for seg in range(segs):
        load(0, seg).start()
    load_metric = pltpu.make_async_copy(metric.at[0, 0], matrix, sem.at[2 * segs])
    load_metric.start()
    for seg in range(segs):
        load(1, seg).start()

    position = 1
    for even, odd in plan:
        if even == odd:
            table[block ^ even] = tiles[position][...]
            position += 1
        else:
            table[block ^ jnp.where(core == 0, even, odd)] = tiles[position][...]
            table[block ^ jnp.where(core == 0, odd, even)] = tiles[position + 1][...]
            position += 2
    for copy in index_loads + [own_tile]:
        copy.wait()
    for source, chosen in enumerate((pattern, pattern_other)):
        for slot in range(slots):
            dens[source, :, slot * width : (slot + 1) * width] = table[chosen[0, 0, slot]]

    out[...] = jnp.zeros_like(out)
    waited = []
    for source in range(2):
        origin = core if source == 0 else 1 - core
        for seg in range(segs):
            load(source, seg).wait()
            if not waited:
                load_metric.wait()
                waited.append(True)

            @pl.when(owner[0, domain[0, origin, seg]] == core)
            def _():
                wide = rows[source, seg].reshape(slots * width, aux)
                half = jnp.dot(dens[source], wide, preferred_element_type=jnp.float32).astype(jnp.bfloat16)
                fitted = jnp.dot(half, matrix[...], preferred_element_type=jnp.float32).astype(jnp.bfloat16)
                out[0, 0] += lax.dot_general(
                    fitted, half, (((1,), (1,)), ((), ())), preferred_element_type=jnp.float32
                )


def local(count, density, three_centre, pattern, domain, owner, metric):
    nocc = density.shape[0]
    slots, width = three_centre.shape[2:4]
    segs, aux = domain.shape[2], metric.shape[2]
    plan = routes(count)
    received = [between_blocks(density, count, even, odd) for even, odd in plan]
    pattern_other = swap_cores(pattern)
    centre_other = swap_cores(three_centre)
    tiles = [density]
    for (even, odd), tile in zip(plan, received):
        tiles.append(tile)
        if even != odd:
            tiles.append(swap_cores(tile))
    vmem = pl.BlockSpec(memory_space=pltpu.VMEM)
    hbm = pl.BlockSpec(memory_space=pltpu.HBM)
    return pl.pallas_call(
        functools.partial(exchange_kernel, plan, count),
        out_shape=jax.ShapeDtypeStruct((1, 1, nocc, nocc), jnp.float32),
        in_specs=[hbm] * 5 + [vmem] * (count - 1) + [hbm] * 3,
        out_specs=vmem,
        scratch_shapes=[
            pltpu.VMEM((count, nocc, width), jnp.bfloat16),
            pltpu.VMEM((2, nocc, slots * width), jnp.bfloat16),
            pltpu.VMEM((2, segs, slots, width, aux), jnp.bfloat16),
            pltpu.VMEM((aux, aux), jnp.bfloat16),
            pltpu.SemaphoreType.DMA((2 * segs + 1,)),
            pltpu.SMEM(pattern.shape, jnp.int32),
            pltpu.SMEM(pattern.shape, jnp.int32),
            pltpu.SMEM(domain.shape, jnp.int32),
            pltpu.SMEM(owner.shape, jnp.int32),
            pltpu.SemaphoreType.DMA((5,)),
        ],
        compiler_params=pltpu.CompilerParams(vmem_limit_bytes=40 * 1024 * 1024),
    )(
        far(pattern), pattern_other, far(domain), far(owner), far(density), *tiles[1:],
        far(three_centre), centre_other, far(metric),
    )


def solution(mesh):
    in_specs = (
        P("groups", "blk"),
        P(("groups", "blk"), "atoms", None, None, None),
        P(("groups", "blk"), "atoms", None),
        P(("groups", "blk"), None, None),
        P(("groups", "blk"), None),
        P(("groups", "blk"), "atoms", None, None),
    )
    out_specs = P(("groups", "blk"), "atoms", None, None)
    body = functools.partial(local, mesh.shape["blk"])
    return jax.shard_map(body, mesh=mesh, in_specs=in_specs, out_specs=out_specs, check_vma=False)
```

```python
import functools
import jax
import jax.numpy as jnp
from jax import lax
from jax.experimental import pallas as pl
from jax.experimental.pallas import tpu as pltpu
from jax.sharding import PartitionSpec as P

AXES = ("blk", "atoms")
TRANSPOSED = (((1,), (1,)), ((), ()))


def between_blocks(block, count, even, odd):
    pairs = []
    for b in range(count):
        pairs.append((2 * b, 2 * (b ^ even)))
        pairs.append((2 * b + 1, 2 * (b ^ odd) + 1))
    return lax.ppermute(block, AXES, pairs)


def swap_cores(block):
    return lax.ppermute(block, "atoms", [(0, 1), (1, 0)])


def far(array):
    return pltpu.with_memory_space_constraint(array, pltpu.HBM)


def routes(count):
    return [(k, k - 1) for k in range(count - 1, 2, -2)] + [(1, 1)]


def stage_kernel(centre, metric, rows, matrix, sem):
    copies = [
        pltpu.make_async_copy(centre.at[0, 0], rows, sem.at[0]),
        pltpu.make_async_copy(metric.at[0, 0], matrix, sem.at[1]),
    ]
    for copy in copies:
        copy.start()
    for copy in copies:
        copy.wait()


def exchange_kernel(plan, count, *refs):
    indices_hbm = refs[:4]
    tiles = refs[4 : 4 + count]
    rows, rows_other, matrix, out = refs[4 + count : 8 + count]
    table, dens = refs[8 + count : 10 + count]
    indices = refs[10 + count : 14 + count]
    sem = refs[14 + count]
    pattern, pattern_other, domain, owner = indices
    block = lax.axis_index("blk")
    core = lax.axis_index("atoms")
    segs = domain.shape[2]
    slots, width = rows.shape[0], rows.shape[1]
    aux = matrix.shape[1]
    nocc = dens.shape[1]

    copies = [
        pltpu.make_async_copy(away, near, sem.at[i]) for i, (away, near) in enumerate(zip(indices_hbm, indices))
    ]
    copies.append(pltpu.make_async_copy(tiles[0], table.at[block], sem.at[4]))
    for copy in copies:
        copy.start()
    position = 1
    for even, odd in plan:
        if even == odd:
            table[block ^ even] = tiles[position][...]
            position += 1
        else:
            table[block ^ jnp.where(core == 0, even, odd)] = tiles[position][...]
            table[block ^ jnp.where(core == 0, odd, even)] = tiles[position + 1][...]
            position += 2
    for copy in copies:
        copy.wait()
    for source, chosen in enumerate((pattern, pattern_other)):
        for slot in range(slots):
            dens[source, :, slot * width : (slot + 1) * width] = table[chosen[0, 0, slot]]

    def halves(source, first, number):
        centre = (rows, rows_other.at[0, 0])[source]
        wide = centre[:, :, first * aux : (first + number) * aux].reshape(slots * width, number * aux)
        return jnp.dot(dens[source], wide, preferred_element_type=jnp.float32).astype(jnp.bfloat16)

    def fit(stack):
        return jnp.dot(stack, matrix[...], preferred_element_type=jnp.float32).astype(jnp.bfloat16)

    out[...] = jnp.zeros_like(out)
    for source in range(2):
        origin = core if source == 0 else 1 - core
        mine = [owner[0, domain[0, origin, seg]] == core for seg in range(segs)]
        every = functools.reduce(jnp.logical_and, mine)

        @pl.when(every)
        def _():
            half = halves(source, 0, segs)
            parts = [half[:, seg * aux : (seg + 1) * aux] for seg in range(segs)]
            fitted = fit(jnp.concatenate(parts, 0))
            total = out[0, 0]
            for seg, part in enumerate(parts):
                total += lax.dot_general(
                    fitted[seg * nocc : (seg + 1) * nocc], part, TRANSPOSED, preferred_element_type=jnp.float32
                )
            out[0, 0] = total

        for seg in range(segs):

            @pl.when(mine[seg] & ~every)
            def _():
                half = halves(source, seg, 1)
                out[0, 0] += lax.dot_general(fit(half), half, TRANSPOSED, preferred_element_type=jnp.float32)


def local(count, density, three_centre, pattern, domain, owner, metric):
    nocc = density.shape[0]
    slots, width = three_centre.shape[2:4]
    aux = metric.shape[2]
    plan = routes(count)
    received = [between_blocks(density, count, even, odd) for even, odd in plan]
    centre_other = swap_cores(three_centre)
    vmem = pl.BlockSpec(memory_space=pltpu.VMEM)
    hbm = pl.BlockSpec(memory_space=pltpu.HBM)
    limit = 24 * 1024 * 1024
    rows, matrix = pl.pallas_call(
        stage_kernel,
        out_shape=(
            jax.ShapeDtypeStruct(three_centre.shape[2:], three_centre.dtype),
            jax.ShapeDtypeStruct(metric.shape[2:], metric.dtype),
        ),
        in_specs=[hbm] * 2,
        out_specs=[vmem] * 2,
        scratch_shapes=[pltpu.SemaphoreType.DMA((2,))],
        compiler_params=pltpu.CompilerParams(vmem_limit_bytes=limit),
    )(far(three_centre), far(metric))
    for k in range(len(received)):
        received[k], rows = lax.optimization_barrier((received[k], rows))
    for k in range(1, len(received)):
        received[k], received[k - 1] = lax.optimization_barrier((received[k], received[k - 1]))
    tiles = [density]
    for (even, odd), tile in zip(plan, received):
        tiles.append(tile)
        if even != odd:
            tiles.append(swap_cores(tile))
    late_pattern, _ = lax.optimization_barrier((pattern, rows))
    pattern_other = swap_cores(late_pattern)
    return pl.pallas_call(
        functools.partial(exchange_kernel, plan, count),
        out_shape=jax.ShapeDtypeStruct((1, 1, nocc, nocc), jnp.float32),
        in_specs=[hbm] * 5 + [vmem] * (count + 2),
        out_specs=vmem,
        scratch_shapes=[
            pltpu.VMEM((count, nocc, width), jnp.bfloat16),
            pltpu.VMEM((2, nocc, slots * width), jnp.bfloat16),
            pltpu.SMEM(pattern.shape, jnp.int32),
            pltpu.SMEM(pattern.shape, jnp.int32),
            pltpu.SMEM(domain.shape, jnp.int32),
            pltpu.SMEM(owner.shape, jnp.int32),
            pltpu.SemaphoreType.DMA((5,)),
        ],
        compiler_params=pltpu.CompilerParams(vmem_limit_bytes=limit),
    )(
        far(pattern), pattern_other, far(domain), far(owner), far(density), *tiles[1:],
        rows, centre_other, matrix,
    )


def solution(mesh):
    in_specs = (
        P("groups", "blk"),
        P(("groups", "blk"), "atoms", None, None, None),
        P(("groups", "blk"), "atoms", None),
        P(("groups", "blk"), None, None),
        P(("groups", "blk"), None),
        P(("groups", "blk"), "atoms", None, None),
    )
    out_specs = P(("groups", "blk"), "atoms", None, None)
    body = functools.partial(local, mesh.shape["blk"])
    return jax.shard_map(body, mesh=mesh, in_specs=in_specs, out_specs=out_specs, check_vma=False)
```

```python
import functools
import jax
import jax.numpy as jnp
from jax import lax
from jax.experimental import pallas as pl
from jax.experimental.pallas import tpu as pltpu
from jax.sharding import PartitionSpec as P

AXES = ("blk", "atoms")
TRANSPOSED = (((1,), (1,)), ((), ()))


def between_blocks(block, even, odd):
    pairs = []
    for targets, core in ((even, 0), (odd, 1)):
        pairs += [(2 * b + core, 2 * target + core) for b, target in enumerate(targets)]
    return lax.ppermute(block, AXES, pairs)


def swap_cores(block):
    return lax.ppermute(block, "atoms", [(0, 1), (1, 0)])


def far(array):
    return pltpu.with_memory_space_constraint(array, pltpu.HBM)


EIGHT = (
    ((3, 4, 5, 2, 1, 6, 7, 0), (4, 3, 6, 7, 2, 1, 0, 5), (1, 0, 3, 5, 6, 7, 2, 4), (2, 5, 0, 1, 7, 3, 4, 6)),
    ((6, 2, 7, 4, 5, 0, 1, 3), (5, 7, 4, 6, 0, 2, 3, 1), (7, 6, 1, 0, 3, 4, 5, 2), ()),
)


def routes(count):
    if count == 8:
        return list(zip(*EIGHT))
    offsets = list(range(count - 1, 0, -1))
    steps = []
    for k in range(0, count - 1, 2):
        even = tuple((b + offsets[k]) % count for b in range(count))
        odd = tuple((b + offsets[k + 1]) % count for b in range(count)) if k + 1 < len(offsets) else ()
        steps.append((even, odd))
    return steps


def origin_of(targets, count, block):
    if not targets:
        return jnp.int32(count)
    origin = jnp.int32(0)
    for b, target in enumerate(targets):
        origin = jnp.where(block == target, b, origin)
    return origin


def stage_kernel(*refs):
    (density, centre, metric), indices_far = refs[:3], refs[3:6]
    own, rows, matrix, message, control = refs[6:11]
    indices, sem = refs[11:14], refs[14]
    pattern, domain, owner = indices
    copies = [pltpu.make_async_copy(away, near, sem.at[i]) for i, (away, near) in enumerate(zip(indices_far, indices))]
    loads = [
        pltpu.make_async_copy(density, own, sem.at[3]),
        pltpu.make_async_copy(centre.at[0, 0], rows, sem.at[4]),
        pltpu.make_async_copy(metric.at[0, 0], matrix, sem.at[5]),
    ]
    for copy in copies + loads:
        copy.start()
    for copy in copies:
        copy.wait()
    core = lax.axis_index("atoms")
    segs, slots = domain.shape[2], pattern.shape[2]
    line = lax.broadcasted_iota(jnp.int32, message.shape, 0)
    chosen = jnp.zeros(message.shape, jnp.int32)
    for slot in range(slots):
        chosen = jnp.where(line == slot, pattern[0, 0, slot], chosen)
    message[...] = chosen.astype(jnp.float32).astype(message.dtype)
    line = lax.broadcasted_iota(jnp.int32, control.shape, 0)
    mine = jnp.zeros(control.shape, jnp.int32)
    for source in range(2):
        origin = core if source == 0 else 1 - core
        for seg in range(segs):
            target = owner[0, domain[0, origin, seg]]
            mine = jnp.where(line == source * segs + seg, jnp.where(target == core, 1, 0), mine)
    control[...] = mine
    for load in loads:
        load.wait()


def exchange_kernel(plan, count, own, packed, swapped, message, control, rows, rows_other, matrix, out, table, dens):
    block = lax.axis_index("blk")
    core = lax.axis_index("atoms")
    slots, width = rows.shape[0], rows.shape[1]
    aux = matrix.shape[1]
    segs = rows.shape[2] // aux
    nocc = dens.shape[1]
    end = nocc * len(plan)

    def slot_numbers(lines):
        values = lines.astype(jnp.float32)
        return [jnp.max(values[slot : slot + 1]).astype(jnp.int32) for slot in range(slots)]

    chosen_by = [slot_numbers(message[...]), slot_numbers(swapped[end:])]
    table[block] = own[...]
    for step, targets in enumerate(plan):
        origins = [origin_of(side, count, block) for side in targets]
        span = slice(step * nocc, (step + 1) * nocc)
        table[jnp.where(core == 0, origins[0], origins[1])] = packed[span]
        table[jnp.where(core == 0, origins[1], origins[0])] = swapped[span]
    for source, chosen in enumerate(chosen_by):
        for slot in range(slots):
            dens[source, :, slot * width : (slot + 1) * width] = table[chosen[slot]]
    flags = control[...].astype(jnp.float32)
    targeted = [jnp.max(flags[i : i + 1]) > 0.5 for i in range(2 * segs)]

    def halves(source, first, number):
        centre = (rows, rows_other.at[0, 0])[source]
        wide = centre[:, :, first * aux : (first + number) * aux].reshape(slots * width, number * aux)
        return jnp.dot(dens[source], wide, preferred_element_type=jnp.float32).astype(jnp.bfloat16)

    def fit(stack):
        return jnp.dot(stack, matrix[...], preferred_element_type=jnp.float32).astype(jnp.bfloat16)

    out[...] = jnp.zeros_like(out)
    for source in range(2):
        mine = targeted[source * segs : (source + 1) * segs]
        every = functools.reduce(jnp.logical_and, mine)

        @pl.when(every)
        def _():
            half = halves(source, 0, segs)
            parts = [half[:, seg * aux : (seg + 1) * aux] for seg in range(segs)]
            fitted = fit(jnp.concatenate(parts, 0))
            total = out[0, 0]
            for seg, part in enumerate(parts):
                total += lax.dot_general(
                    fitted[seg * nocc : (seg + 1) * nocc], part, TRANSPOSED, preferred_element_type=jnp.float32
                )
            out[0, 0] = total

        for seg in range(segs):

            @pl.when(mine[seg] & ~every)
            def _():
                half = halves(source, seg, 1)
                out[0, 0] += lax.dot_general(fit(half), half, TRANSPOSED, preferred_element_type=jnp.float32)


def local(count, density, three_centre, pattern, domain, owner, metric):
    nocc = density.shape[0]
    slots, width = three_centre.shape[2:4]
    segs = domain.shape[2]
    plan = routes(count)
    received = [between_blocks(density, even, odd) for even, odd in plan]
    centre_other = swap_cores(three_centre)
    vmem = pl.BlockSpec(memory_space=pltpu.VMEM)
    hbm = pl.BlockSpec(memory_space=pltpu.HBM)
    limit = 24 * 1024 * 1024
    lines = -(-slots // 16) * 16
    own, rows, matrix, message, control = pl.pallas_call(
        stage_kernel,
        out_shape=(
            jax.ShapeDtypeStruct(density.shape, density.dtype),
            jax.ShapeDtypeStruct(three_centre.shape[2:], three_centre.dtype),
            jax.ShapeDtypeStruct(metric.shape[2:], metric.dtype),
            jax.ShapeDtypeStruct((lines, width), density.dtype),
            jax.ShapeDtypeStruct((-(-2 * segs // 8) * 8, 128), jnp.int32),
        ),
        in_specs=[hbm] * 6,
        out_specs=[vmem] * 5,
        scratch_shapes=[
            pltpu.SMEM(pattern.shape, jnp.int32),
            pltpu.SMEM(domain.shape, jnp.int32),
            pltpu.SMEM(owner.shape, jnp.int32),
            pltpu.SemaphoreType.DMA((6,)),
        ],
        compiler_params=pltpu.CompilerParams(vmem_limit_bytes=limit),
    )(*[far(array) for array in (density, three_centre, metric, pattern, domain, owner)])
    for k in range(len(received)):
        received[k], message = lax.optimization_barrier((received[k], message))
    packed = jnp.concatenate(received + [message], 0)
    swapped = swap_cores(packed)
    return pl.pallas_call(
        functools.partial(exchange_kernel, plan, count),
        out_shape=jax.ShapeDtypeStruct((1, 1, nocc, nocc), jnp.float32),
        in_specs=[vmem] * 8,
        out_specs=vmem,
        scratch_shapes=[
            pltpu.VMEM((count + 1, nocc, width), jnp.bfloat16),
            pltpu.VMEM((2, nocc, slots * width), jnp.bfloat16),
        ],
        compiler_params=pltpu.CompilerParams(vmem_limit_bytes=limit),
    )(own, packed, swapped, message, control, rows, centre_other, matrix)


def solution(mesh):
    in_specs = (
        P("groups", "blk"),
        P(("groups", "blk"), "atoms", None, None, None),
        P(("groups", "blk"), "atoms", None),
        P(("groups", "blk"), None, None),
        P(("groups", "blk"), None),
        P(("groups", "blk"), "atoms", None, None),
    )
    out_specs = P(("groups", "blk"), "atoms", None, None)
    body = functools.partial(local, mesh.shape["blk"])
    return jax.shard_map(body, mesh=mesh, in_specs=in_specs, out_specs=out_specs, check_vma=False)
```

```python
import functools
import jax
import jax.numpy as jnp
from jax import lax
from jax.experimental import pallas as pl
from jax.experimental.pallas import tpu as pltpu
from jax.sharding import PartitionSpec as P

AXES = ("blk", "atoms")
TRANSPOSED = (((1,), (1,)), ((), ()))
BLOCK = 256


def between_blocks(block, even, odd):
    pairs = []
    for targets, core in ((even, 0), (odd, 1)):
        pairs += [(2 * b + core, 2 * target + core) for b, target in enumerate(targets)]
    return lax.ppermute(block, AXES, pairs)


def swap_cores(block):
    return lax.ppermute(block, "atoms", [(0, 1), (1, 0)])


def far(array):
    return pltpu.with_memory_space_constraint(array, pltpu.HBM)


EIGHT = (
    ((3, 4, 5, 2, 1, 6, 7, 0), (4, 3, 6, 7, 2, 1, 0, 5), (1, 0, 3, 5, 6, 7, 2, 4), (2, 5, 0, 1, 7, 3, 4, 6)),
    ((6, 2, 7, 4, 5, 0, 1, 3), (5, 7, 4, 6, 0, 2, 3, 1), (7, 6, 1, 0, 3, 4, 5, 2), ()),
)


def routes(count):
    if count == 8:
        return list(zip(*EIGHT))
    offsets = list(range(count - 1, 0, -1))
    steps = []
    for k in range(0, count - 1, 2):
        even = tuple((b + offsets[k]) % count for b in range(count))
        odd = tuple((b + offsets[k + 1]) % count for b in range(count)) if k + 1 < len(offsets) else ()
        steps.append((even, odd))
    return steps


def origin_of(targets, count, block):
    if not targets:
        return jnp.int32(count)
    origin = jnp.int32(0)
    for b, target in enumerate(targets):
        origin = jnp.where(block == target, b, origin)
    return origin


def stage_kernel(*refs):
    (density, centre, metric), indices_far = refs[:3], refs[3:6]
    own, rows, matrix, message, control = refs[6:11]
    indices, sem = refs[11:14], refs[14]
    pattern, domain, owner = indices
    copies = [pltpu.make_async_copy(away, near, sem.at[i]) for i, (away, near) in enumerate(zip(indices_far, indices))]
    loads = [
        pltpu.make_async_copy(density, own, sem.at[3]),
        pltpu.make_async_copy(centre.at[0, 0], rows, sem.at[4]),
        pltpu.make_async_copy(metric.at[0, 0], matrix, sem.at[5]),
    ]
    for copy in copies + loads:
        copy.start()
    for copy in copies:
        copy.wait()
    core = lax.axis_index("atoms")
    segs, slots = domain.shape[2], pattern.shape[2]
    line = lax.broadcasted_iota(jnp.int32, message.shape, 0)
    chosen = jnp.zeros(message.shape, jnp.int32)
    for slot in range(slots):
        chosen = jnp.where(line == slot, pattern[0, 0, slot], chosen)
    message[...] = chosen.astype(jnp.float32).astype(message.dtype)
    line = lax.broadcasted_iota(jnp.int32, control.shape, 0)
    mine = jnp.zeros(control.shape, jnp.int32)
    for source in range(2):
        origin = core if source == 0 else 1 - core
        for seg in range(segs):
            target = owner[0, domain[0, origin, seg]]
            mine = jnp.where(line == source * segs + seg, jnp.where(target == core, 1, 0), mine)
    control[...] = mine
    for load in loads:
        load.wait()


def exchange_kernel(plan, count, own, packed, swapped, message, control, rows, rows_other, matrix, out, table, dens, total_ref):
    block = lax.axis_index("blk")
    core = lax.axis_index("atoms")
    slots, width = rows.shape[0], rows.shape[1]
    aux = matrix.shape[1]
    segs = rows.shape[2] // aux
    nocc = dens.shape[1]
    end = nocc * len(plan)

    def slot_numbers(lines):
        values = lines.astype(jnp.float32)
        return [jnp.max(values[slot : slot + 1]).astype(jnp.int32) for slot in range(slots)]

    chosen_by = [slot_numbers(message[...]), slot_numbers(swapped[end:])]
    table[block] = own[...]
    for step, targets in enumerate(plan):
        origins = [origin_of(side, count, block) for side in targets]
        span = slice(step * nocc, (step + 1) * nocc)
        table[jnp.where(core == 0, origins[0], origins[1])] = packed[span]
        table[jnp.where(core == 0, origins[1], origins[0])] = swapped[span]
    for source, chosen in enumerate(chosen_by):
        for slot in range(slots):
            dens[source, :, slot * width : (slot + 1) * width] = table[chosen[slot]]
    flags = control[...].astype(jnp.float32)
    targeted = [jnp.max(flags[i : i + 1]) > 0.5 for i in range(2 * segs)]

    def halves(source, first, number):
        centre = (rows, rows_other.at[0, 0])[source]
        wide = centre[:, :, first * aux : (first + number) * aux].reshape(slots * width, number * aux)
        return jnp.dot(dens[source], wide, preferred_element_type=jnp.float32).astype(jnp.bfloat16)

    def lower_product(parts):
        total = jnp.zeros((nocc, nocc), jnp.float32)
        stack = jnp.concatenate(parts, 0)
        columns = [0.0] * (aux // BLOCK)
        for i in range(aux // BLOCK):
            lines = slice(i * BLOCK, (i + 1) * BLOCK)
            wide = jnp.dot(stack[:, lines], matrix[lines, i * BLOCK :], preferred_element_type=jnp.float32)
            for j in range(i, aux // BLOCK):
                piece = wide[:, (j - i) * BLOCK : (j - i + 1) * BLOCK]
                columns[j] += 0.5 * piece if i == j else piece
        for i, column in enumerate(columns):
            fitted = column.astype(jnp.bfloat16)
            for seg, part in enumerate(parts):
                total += lax.dot_general(
                    fitted[seg * nocc : (seg + 1) * nocc], part[:, i * BLOCK : (i + 1) * BLOCK], TRANSPOSED,
                    preferred_element_type=jnp.float32,
                )
        return total

    total_ref[...] = jnp.zeros_like(total_ref)
    for source in range(2):
        mine = targeted[source * segs : (source + 1) * segs]
        every = functools.reduce(jnp.logical_and, mine)

        @pl.when(every)
        def _():
            half = halves(source, 0, segs)
            total_ref[...] += lower_product([half[:, seg * aux : (seg + 1) * aux] for seg in range(segs)])

        for seg in range(segs):

            @pl.when(mine[seg] & ~every)
            def _():
                total_ref[...] += lower_product([halves(source, seg, 1)])

    out[0, 0] = total_ref[...] + total_ref[...].T


def local(count, density, three_centre, pattern, domain, owner, metric):
    nocc = density.shape[0]
    slots, width = three_centre.shape[2:4]
    segs = domain.shape[2]
    plan = routes(count)
    received = [between_blocks(density, even, odd) for even, odd in plan]
    centre_other = swap_cores(three_centre)
    vmem = pl.BlockSpec(memory_space=pltpu.VMEM)
    hbm = pl.BlockSpec(memory_space=pltpu.HBM)
    limit = 24 * 1024 * 1024
    lines = -(-slots // 16) * 16
    own, rows, matrix, message, control = pl.pallas_call(
        stage_kernel,
        out_shape=(
            jax.ShapeDtypeStruct(density.shape, density.dtype),
            jax.ShapeDtypeStruct(three_centre.shape[2:], three_centre.dtype),
            jax.ShapeDtypeStruct(metric.shape[2:], metric.dtype),
            jax.ShapeDtypeStruct((lines, width), density.dtype),
            jax.ShapeDtypeStruct((-(-2 * segs // 8) * 8, 128), jnp.int32),
        ),
        in_specs=[hbm] * 6,
        out_specs=[vmem] * 5,
        scratch_shapes=[
            pltpu.SMEM(pattern.shape, jnp.int32),
            pltpu.SMEM(domain.shape, jnp.int32),
            pltpu.SMEM(owner.shape, jnp.int32),
            pltpu.SemaphoreType.DMA((6,)),
        ],
        compiler_params=pltpu.CompilerParams(vmem_limit_bytes=limit),
    )(*[far(array) for array in (density, three_centre, metric, pattern, domain, owner)])
    for k in range(len(received)):
        received[k], message = lax.optimization_barrier((received[k], message))
    packed = jnp.concatenate(received + [message], 0)
    swapped = swap_cores(packed)
    return pl.pallas_call(
        functools.partial(exchange_kernel, plan, count),
        out_shape=jax.ShapeDtypeStruct((1, 1, nocc, nocc), jnp.float32),
        in_specs=[vmem] * 8,
        out_specs=vmem,
        scratch_shapes=[
            pltpu.VMEM((count + 1, nocc, width), jnp.bfloat16),
            pltpu.VMEM((2, nocc, slots * width), jnp.bfloat16),
            pltpu.VMEM((nocc, nocc), jnp.float32),
        ],
        compiler_params=pltpu.CompilerParams(vmem_limit_bytes=limit),
    )(own, packed, swapped, message, control, rows, centre_other, matrix)


def solution(mesh):
    in_specs = (
        P("groups", "blk"),
        P(("groups", "blk"), "atoms", None, None, None),
        P(("groups", "blk"), "atoms", None),
        P(("groups", "blk"), None, None),
        P(("groups", "blk"), None),
        P(("groups", "blk"), "atoms", None, None),
    )
    out_specs = P(("groups", "blk"), "atoms", None, None)
    body = functools.partial(local, mesh.shape["blk"])
    return jax.shard_map(body, mesh=mesh, in_specs=in_specs, out_specs=out_specs, check_vma=False)
```

```python
import functools
import jax
import jax.numpy as jnp
from jax import lax
from jax.experimental import pallas as pl
from jax.experimental.pallas import tpu as pltpu
from jax.sharding import PartitionSpec as P

AXES = ("blk", "atoms")
TRANSPOSED = (((1,), (1,)), ((), ()))
BLOCK = 256


def between_blocks(block, even, odd):
    pairs = []
    for targets, core in ((even, 0), (odd, 1)):
        pairs += [(2 * b + core, 2 * target + core) for b, target in enumerate(targets)]
    return lax.ppermute(block, AXES, pairs)


def swap_cores(block):
    return lax.ppermute(block, "atoms", [(0, 1), (1, 0)])


def far(array):
    return pltpu.with_memory_space_constraint(array, pltpu.HBM)


EIGHT = (
    ((3, 4, 5, 2, 1, 6, 7, 0), (4, 3, 6, 7, 2, 1, 0, 5), (1, 0, 3, 5, 6, 7, 2, 4), (2, 5, 0, 1, 7, 3, 4, 6)),
    ((6, 2, 7, 4, 5, 0, 1, 3), (5, 7, 4, 6, 0, 2, 3, 1), (7, 6, 1, 0, 3, 4, 5, 2), (1, 0, 3, 2, 5, 4, 7, 6)),
)


def routes(count):
    if count == 8:
        return list(zip(*EIGHT))
    offsets = list(range(count - 1, 0, -1))
    steps = []
    for k in range(0, count - 1, 2):
        even = tuple((b + offsets[k]) % count for b in range(count))
        odd = tuple((b + offsets[k + 1]) % count for b in range(count)) if k + 1 < len(offsets) else ()
        steps.append((even, odd))
    return steps


def origin_of(targets, count, block):
    if not targets:
        return jnp.int32(count)
    origin = jnp.int32(0)
    for b, target in enumerate(targets):
        origin = jnp.where(block == target, b, origin)
    return origin


def stage_kernel(*refs):
    (density, centre, metric), indices_far = refs[:3], refs[3:6]
    own, rows, matrix, message, control = refs[6:11]
    indices, sem = refs[11:14], refs[14]
    pattern, domain, owner = indices
    copies = [pltpu.make_async_copy(away, near, sem.at[i]) for i, (away, near) in enumerate(zip(indices_far, indices))]
    loads = [
        pltpu.make_async_copy(density, own, sem.at[3]),
        pltpu.make_async_copy(centre.at[0, 0], rows, sem.at[4]),
        pltpu.make_async_copy(metric.at[0, 0], matrix, sem.at[5]),
    ]
    for copy in copies + loads:
        copy.start()
    for copy in copies:
        copy.wait()
    core = lax.axis_index("atoms")
    segs, slots = domain.shape[2], pattern.shape[2]
    line = lax.broadcasted_iota(jnp.int32, message.shape, 0)
    chosen = jnp.zeros(message.shape, jnp.int32)
    for slot in range(slots):
        chosen = jnp.where(line == slot, pattern[0, 0, slot], chosen)
    message[...] = chosen.astype(jnp.float32).astype(message.dtype)
    line = lax.broadcasted_iota(jnp.int32, control.shape, 0)
    mine = jnp.zeros(control.shape, jnp.int32)
    for source in range(2):
        origin = core if source == 0 else 1 - core
        for seg in range(segs):
            target = owner[0, domain[0, origin, seg]]
            mine = jnp.where(line == source * segs + seg, jnp.where(target == core, 1, 0), mine)
    control[...] = mine
    for load in loads:
        load.wait()


def exchange_kernel(plan, count, own, packed, swapped, message, control, rows, rows_other, matrix, out, table, dens, total_ref):
    block = lax.axis_index("blk")
    core = lax.axis_index("atoms")
    slots, width = rows.shape[0], rows.shape[1]
    aux = matrix.shape[1]
    segs = rows.shape[2] // aux
    nocc = dens.shape[1]
    end = nocc * len(plan)

    def slot_numbers(lines):
        values = lines.astype(jnp.float32)
        return [jnp.max(values[slot : slot + 1]).astype(jnp.int32) for slot in range(slots)]

    chosen_by = [slot_numbers(message[...]), slot_numbers(swapped[end:])]
    table[block] = own[...]
    for step, targets in enumerate(plan):
        origins = [origin_of(side, count, block) for side in targets]
        span = slice(step * nocc, (step + 1) * nocc)
        table[jnp.where(core == 0, origins[0], origins[1])] = packed[span]
        table[jnp.where(core == 0, origins[1], origins[0])] = swapped[span]
    for source, chosen in enumerate(chosen_by):
        for slot in range(slots):
            dens[source, :, slot * width : (slot + 1) * width] = table[chosen[slot]]
    flags = control[...].astype(jnp.float32)
    targeted = [jnp.max(flags[i : i + 1]) > 0.5 for i in range(2 * segs)]

    def halves(source, first, number):
        centre = (rows, rows_other.at[0, 0])[source]
        wide = centre[:, :, first * aux : (first + number) * aux].reshape(slots * width, number * aux)
        return jnp.dot(dens[source], wide, preferred_element_type=jnp.float32).astype(jnp.bfloat16)

    def lower_product(parts):
        total = jnp.zeros((nocc, nocc), jnp.float32)
        stack = jnp.concatenate(parts, 0)
        columns = [0.0] * (aux // BLOCK)
        for i in range(aux // BLOCK):
            lines = slice(i * BLOCK, (i + 1) * BLOCK)
            wide = jnp.dot(stack[:, lines], matrix[lines, i * BLOCK :], preferred_element_type=jnp.float32)
            for j in range(i, aux // BLOCK):
                piece = wide[:, (j - i) * BLOCK : (j - i + 1) * BLOCK]
                columns[j] += 0.5 * piece if i == j else piece
        for i, column in enumerate(columns):
            fitted = column.astype(jnp.bfloat16)
            for seg, part in enumerate(parts):
                total += lax.dot_general(
                    fitted[seg * nocc : (seg + 1) * nocc], part[:, i * BLOCK : (i + 1) * BLOCK], TRANSPOSED,
                    preferred_element_type=jnp.float32,
                )
        return total

    total_ref[...] = jnp.zeros_like(total_ref)
    for source in range(2):
        mine = targeted[source * segs : (source + 1) * segs]
        every = functools.reduce(jnp.logical_and, mine)

        @pl.when(every)
        def _():
            half = halves(source, 0, segs)
            total_ref[...] += lower_product([half[:, seg * aux : (seg + 1) * aux] for seg in range(segs)])

        for seg in range(segs):

            @pl.when(mine[seg] & ~every)
            def _():
                total_ref[...] += lower_product([halves(source, seg, 1)])

    out[0, 0] = total_ref[...] + total_ref[...].T


def local(count, density, three_centre, pattern, domain, owner, metric):
    nocc = density.shape[0]
    slots, width = three_centre.shape[2:4]
    segs = domain.shape[2]
    plan = routes(count)
    received = [between_blocks(density, even, odd) for even, odd in plan]
    centre_other = swap_cores(three_centre)
    vmem = pl.BlockSpec(memory_space=pltpu.VMEM)
    hbm = pl.BlockSpec(memory_space=pltpu.HBM)
    limit = 24 * 1024 * 1024
    lines = -(-slots // 16) * 16
    own, rows, matrix, message, control = pl.pallas_call(
        stage_kernel,
        out_shape=(
            jax.ShapeDtypeStruct(density.shape, density.dtype),
            jax.ShapeDtypeStruct(three_centre.shape[2:], three_centre.dtype),
            jax.ShapeDtypeStruct(metric.shape[2:], metric.dtype),
            jax.ShapeDtypeStruct((lines, width), density.dtype),
            jax.ShapeDtypeStruct((-(-2 * segs // 8) * 8, 128), jnp.int32),
        ),
        in_specs=[hbm] * 6,
        out_specs=[vmem] * 5,
        scratch_shapes=[
            pltpu.SMEM(pattern.shape, jnp.int32),
            pltpu.SMEM(domain.shape, jnp.int32),
            pltpu.SMEM(owner.shape, jnp.int32),
            pltpu.SemaphoreType.DMA((6,)),
        ],
        compiler_params=pltpu.CompilerParams(vmem_limit_bytes=limit),
    )(*[far(array) for array in (density, three_centre, metric, pattern, domain, owner)])
    for k in range(len(received)):
        received[k], message = lax.optimization_barrier((received[k], message))
    packed = jnp.concatenate(received + [message], 0)
    swapped = swap_cores(packed)
    return pl.pallas_call(
        functools.partial(exchange_kernel, plan, count),
        out_shape=jax.ShapeDtypeStruct((1, 1, nocc, nocc), jnp.float32),
        in_specs=[vmem] * 8,
        out_specs=vmem,
        scratch_shapes=[
            pltpu.VMEM((count + 1, nocc, width), jnp.bfloat16),
            pltpu.VMEM((2, nocc, slots * width), jnp.bfloat16),
            pltpu.VMEM((nocc, nocc), jnp.float32),
        ],
        compiler_params=pltpu.CompilerParams(vmem_limit_bytes=limit),
    )(own, packed, swapped, message, control, rows, centre_other, matrix)


def solution(mesh):
    in_specs = (
        P("groups", "blk"),
        P(("groups", "blk"), "atoms", None, None, None),
        P(("groups", "blk"), "atoms", None),
        P(("groups", "blk"), None, None),
        P(("groups", "blk"), None),
        P(("groups", "blk"), "atoms", None, None),
    )
    out_specs = P(("groups", "blk"), "atoms", None, None)
    body = functools.partial(local, mesh.shape["blk"])
    return jax.shard_map(body, mesh=mesh, in_specs=in_specs, out_specs=out_specs, check_vma=False)
```

```python
import functools
import jax
import jax.numpy as jnp
from jax import lax
from jax.experimental import pallas as pl
from jax.experimental.pallas import tpu as pltpu
from jax.sharding import PartitionSpec as P

AXES = ("blk", "atoms")
TRANSPOSED = (((1,), (1,)), ((), ()))
BLOCK = 256


def between_blocks(block, even, odd):
    pairs = []
    for targets, core in ((even, 0), (odd, 1)):
        pairs += [(2 * b + core, 2 * target + core) for b, target in enumerate(targets)]
    return lax.ppermute(block, AXES, pairs)


def swap_cores(block):
    return lax.ppermute(block, "atoms", [(0, 1), (1, 0)])


def far(array):
    return pltpu.with_memory_space_constraint(array, pltpu.HBM)


EIGHT = (
    ((1, 3, 6, 5, 2, 7, 4, 0), (4, 7, 5, 0, 6, 3, 1, 2), (5, 6, 4, 7, 3, 0, 2, 1), (2, 0, 3, 1, 5, 4, 7, 6)),
    ((3, 5, 1, 6, 7, 2, 0, 4), (6, 2, 7, 4, 0, 1, 3, 5), (7, 4, 0, 2, 1, 6, 5, 3), (2, 0, 3, 1, 5, 4, 7, 6)),
)


def routes(count):
    if count == 8:
        return list(zip(EIGHT[0][:3], EIGHT[1][:3])), EIGHT[0][3]
    shifts = [tuple((b + k) % count for b in range(count)) for k in range(count - 1, 1, -1)]
    shared = tuple((b + 1) % count for b in range(count))
    shifts += [shared] * (len(shifts) % 2)
    return list(zip(shifts[::2], shifts[1::2])), shared


def origin_of(targets, count, block):
    origin = jnp.int32(0)
    for b, target in enumerate(targets):
        origin = jnp.where(block == target, b, origin)
    return origin


def stage_kernel(*refs):
    (density, centre, metric), indices_far = refs[:3], refs[3:6]
    own, rows, matrix, message, control = refs[6:11]
    indices, sem = refs[11:14], refs[14]
    pattern, domain, owner = indices
    copies = [pltpu.make_async_copy(away, near, sem.at[i]) for i, (away, near) in enumerate(zip(indices_far, indices))]
    loads = [
        pltpu.make_async_copy(density, own, sem.at[3]),
        pltpu.make_async_copy(centre.at[0, 0], rows, sem.at[4]),
        pltpu.make_async_copy(metric.at[0, 0], matrix, sem.at[5]),
    ]
    for copy in copies + loads:
        copy.start()
    for copy in copies:
        copy.wait()
    core = lax.axis_index("atoms")
    segs, slots = domain.shape[2], pattern.shape[2]
    line = lax.broadcasted_iota(jnp.int32, message.shape, 0)
    chosen = jnp.zeros(message.shape, jnp.int32)
    for slot in range(slots):
        chosen = jnp.where(line == slot, pattern[0, 0, slot], chosen)
    message[...] = chosen.astype(jnp.float32).astype(message.dtype)
    line = lax.broadcasted_iota(jnp.int32, control.shape, 0)
    mine = jnp.zeros(control.shape, jnp.int32)
    for source in range(2):
        origin = core if source == 0 else 1 - core
        for seg in range(segs):
            target = owner[0, domain[0, origin, seg]]
            mine = jnp.where(line == source * segs + seg, jnp.where(target == core, 1, 0), mine)
    control[...] = mine
    for load in loads:
        load.wait()


def hold_kernel(given, taken):
    taken[...] = given[...]


def exchange_kernel(plan, shared, count, own, last, packed, swapped, message, control, rows, rows_other, matrix, out, table, dens, total_ref):
    block = lax.axis_index("blk")
    core = lax.axis_index("atoms")
    slots, width = rows.shape[0], rows.shape[1]
    aux = matrix.shape[1]
    segs = rows.shape[2] // aux
    nocc = dens.shape[1]
    end = nocc * len(plan)

    def slot_numbers(lines):
        values = lines.astype(jnp.float32)
        return [jnp.max(values[slot : slot + 1]).astype(jnp.int32) for slot in range(slots)]

    chosen_by = [slot_numbers(message[...]), slot_numbers(swapped[end:])]
    table[block] = own[...]
    for step, (even, odd) in enumerate(plan):
        near, across = origin_of(even, count, block), origin_of(odd, count, block)
        span = slice(step * nocc, (step + 1) * nocc)
        table[jnp.where(core == 0, near, across)] = packed[span]
        table[jnp.where(core == 0, across, near)] = swapped[span]
    table[origin_of(shared, count, block)] = last[...]
    for source, chosen in enumerate(chosen_by):
        for slot in range(slots):
            dens[source, :, slot * width : (slot + 1) * width] = table[chosen[slot]]
    flags = control[...].astype(jnp.float32)
    targeted = [jnp.max(flags[i : i + 1]) > 0.5 for i in range(2 * segs)]

    def halves(source, first, number):
        centre = (rows, rows_other.at[0, 0])[source]
        wide = centre[:, :, first * aux : (first + number) * aux].reshape(slots * width, number * aux)
        return jnp.dot(dens[source], wide, preferred_element_type=jnp.float32).astype(jnp.bfloat16)

    def lower_product(parts):
        total = jnp.zeros((nocc, nocc), jnp.float32)
        stack = jnp.concatenate(parts, 0)
        columns = [0.0] * (aux // BLOCK)
        for i in range(aux // BLOCK):
            lines = slice(i * BLOCK, (i + 1) * BLOCK)
            wide = jnp.dot(stack[:, lines], matrix[lines, i * BLOCK :], preferred_element_type=jnp.float32)
            for j in range(i, aux // BLOCK):
                piece = wide[:, (j - i) * BLOCK : (j - i + 1) * BLOCK]
                columns[j] += 0.5 * piece if i == j else piece
        for i, column in enumerate(columns):
            fitted = column.astype(jnp.bfloat16)
            for seg, part in enumerate(parts):
                total += lax.dot_general(
                    fitted[seg * nocc : (seg + 1) * nocc], part[:, i * BLOCK : (i + 1) * BLOCK], TRANSPOSED,
                    preferred_element_type=jnp.float32,
                )
        return total

    total_ref[...] = jnp.zeros_like(total_ref)
    for source in range(2):
        mine = targeted[source * segs : (source + 1) * segs]
        every = functools.reduce(jnp.logical_and, mine)

        @pl.when(every)
        def _():
            half = halves(source, 0, segs)
            total_ref[...] += lower_product([half[:, seg * aux : (seg + 1) * aux] for seg in range(segs)])

        for seg in range(segs):

            @pl.when(mine[seg] & ~every)
            def _():
                total_ref[...] += lower_product([halves(source, seg, 1)])

    out[0, 0] = total_ref[...] + total_ref[...].T


def local(count, density, three_centre, pattern, domain, owner, metric):
    nocc = density.shape[0]
    slots, width = three_centre.shape[2:4]
    segs = domain.shape[2]
    plan, shared = routes(count)
    received = [between_blocks(density, even, odd) for even, odd in plan]
    last = between_blocks(density, shared, shared)
    centre_other = swap_cores(three_centre)
    vmem = pl.BlockSpec(memory_space=pltpu.VMEM)
    hbm = pl.BlockSpec(memory_space=pltpu.HBM)
    limit = 24 * 1024 * 1024
    lines = -(-slots // 16) * 16
    own, rows, matrix, message, control = pl.pallas_call(
        stage_kernel,
        out_shape=(
            jax.ShapeDtypeStruct(density.shape, density.dtype),
            jax.ShapeDtypeStruct(three_centre.shape[2:], three_centre.dtype),
            jax.ShapeDtypeStruct(metric.shape[2:], metric.dtype),
            jax.ShapeDtypeStruct((lines, width), density.dtype),
            jax.ShapeDtypeStruct((-(-2 * segs // 8) * 8, 128), jnp.int32),
        ),
        in_specs=[hbm] * 6,
        out_specs=[vmem] * 5,
        scratch_shapes=[
            pltpu.SMEM(pattern.shape, jnp.int32),
            pltpu.SMEM(domain.shape, jnp.int32),
            pltpu.SMEM(owner.shape, jnp.int32),
            pltpu.SemaphoreType.DMA((6,)),
        ],
        compiler_params=pltpu.CompilerParams(vmem_limit_bytes=limit),
    )(*[far(array) for array in (density, three_centre, metric, pattern, domain, owner)])
    for k in range(len(received)):
        received[k], message = lax.optimization_barrier((received[k], message))
    last, _ = lax.optimization_barrier((last, message))
    last = pl.pallas_call(
        hold_kernel,
        out_shape=jax.ShapeDtypeStruct(last.shape, last.dtype),
        in_specs=[vmem],
        out_specs=vmem,
        compiler_params=pltpu.CompilerParams(vmem_limit_bytes=limit),
        cost_estimate=pl.CostEstimate(flops=1400000000, bytes_accessed=2 * last.size * 2, transcendentals=0),
    )(last)
    packed = jnp.concatenate(received + [message], 0)
    swapped = swap_cores(packed)
    return pl.pallas_call(
        functools.partial(exchange_kernel, plan, shared, count),
        out_shape=jax.ShapeDtypeStruct((1, 1, nocc, nocc), jnp.float32),
        in_specs=[vmem] * 9,
        out_specs=vmem,
        scratch_shapes=[
            pltpu.VMEM((count, nocc, width), jnp.bfloat16),
            pltpu.VMEM((2, nocc, slots * width), jnp.bfloat16),
            pltpu.VMEM((nocc, nocc), jnp.float32),
        ],
        compiler_params=pltpu.CompilerParams(vmem_limit_bytes=limit),
    )(own, last, packed, swapped, message, control, rows, centre_other, matrix)


def solution(mesh):
    in_specs = (
        P("groups", "blk"),
        P(("groups", "blk"), "atoms", None, None, None),
        P(("groups", "blk"), "atoms", None),
        P(("groups", "blk"), None, None),
        P(("groups", "blk"), None),
        P(("groups", "blk"), "atoms", None, None),
    )
    out_specs = P(("groups", "blk"), "atoms", None, None)
    body = functools.partial(local, mesh.shape["blk"])
    return jax.shard_map(body, mesh=mesh, in_specs=in_specs, out_specs=out_specs, check_vma=False)
```

```python
import functools
import jax
import jax.numpy as jnp
from jax import lax
from jax.experimental import pallas as pl
from jax.experimental.pallas import tpu as pltpu
from jax.sharding import PartitionSpec as P

AXES = ("blk", "atoms")
TRANSPOSED = (((1,), (1,)), ((), ()))
BLOCK = 256


def between_blocks(block, even, odd):
    pairs = []
    for targets, core in ((even, 0), (odd, 1)):
        pairs += [(2 * b + core, 2 * target + core) for b, target in enumerate(targets)]
    return lax.ppermute(block, AXES, pairs)


def swap_cores(block):
    return lax.ppermute(block, "atoms", [(0, 1), (1, 0)])


def far(array):
    return pltpu.with_memory_space_constraint(array, pltpu.HBM)


EIGHT = (
    ((1, 3, 4, 5, 2, 7, 0, 6), (6, 5, 1, 7, 0, 3, 2, 4), (7, 4, 0, 1, 6, 2, 5, 3), (2, 0, 3, 6, 7, 1, 4, 5)),
    ((3, 6, 7, 4, 5, 0, 1, 2), (4, 7, 5, 2, 1, 6, 3, 0), (5, 2, 6, 0, 3, 4, 7, 1), (2, 0, 3, 6, 7, 1, 4, 5)),
)


def routes(count):
    if count == 8:
        return list(zip(EIGHT[0][:3], EIGHT[1][:3])), EIGHT[0][3]
    shifts = [tuple((b + k) % count for b in range(count)) for k in range(count - 1, 1, -1)]
    shared = tuple((b + 1) % count for b in range(count))
    shifts += [shared] * (len(shifts) % 2)
    return list(zip(shifts[::2], shifts[1::2])), shared


def origin_of(targets, count, block):
    origin = jnp.int32(0)
    for b, target in enumerate(targets):
        origin = jnp.where(block == target, b, origin)
    return origin


def stage_kernel(*refs):
    (density, centre, metric), indices_far = refs[:3], refs[3:6]
    own, rows, matrix, message, control = refs[6:11]
    indices, sem = refs[11:14], refs[14]
    pattern, domain, owner = indices
    copies = [pltpu.make_async_copy(away, near, sem.at[i]) for i, (away, near) in enumerate(zip(indices_far, indices))]
    loads = [
        pltpu.make_async_copy(density, own, sem.at[3]),
        pltpu.make_async_copy(centre.at[0, 0], rows, sem.at[4]),
        pltpu.make_async_copy(metric.at[0, 0], matrix, sem.at[5]),
    ]
    for copy in copies + loads:
        copy.start()
    for copy in copies:
        copy.wait()
    core = lax.axis_index("atoms")
    segs, slots = domain.shape[2], pattern.shape[2]
    line = lax.broadcasted_iota(jnp.int32, message.shape, 0)
    chosen = jnp.zeros(message.shape, jnp.int32)
    for slot in range(slots):
        chosen = jnp.where(line == slot, pattern[0, 0, slot], chosen)
    message[...] = chosen.astype(jnp.float32).astype(message.dtype)
    line = lax.broadcasted_iota(jnp.int32, control.shape, 0)
    mine = jnp.zeros(control.shape, jnp.int32)
    for source in range(2):
        origin = core if source == 0 else 1 - core
        for seg in range(segs):
            target = owner[0, domain[0, origin, seg]]
            mine = jnp.where(line == source * segs + seg, jnp.where(target == core, 1, 0), mine)
    control[...] = mine
    for load in loads:
        load.wait()


def hold_kernel(given, taken):
    taken[...] = given[...]


def exchange_kernel(plan, shared, count, own, last, packed, swapped, message, control, rows, rows_other, matrix, out, table, dens, total_ref):
    block = lax.axis_index("blk")
    core = lax.axis_index("atoms")
    slots, width = rows.shape[0], rows.shape[1]
    aux = matrix.shape[1]
    segs = rows.shape[2] // aux
    nocc = dens.shape[1]
    end = nocc * len(plan)

    def slot_numbers(lines):
        values = lines.astype(jnp.float32)
        return [jnp.max(values[slot : slot + 1]).astype(jnp.int32) for slot in range(slots)]

    chosen_by = [slot_numbers(message[...]), slot_numbers(swapped[end:])]
    table[block] = own[...]
    for step, (even, odd) in enumerate(plan):
        near, across = origin_of(even, count, block), origin_of(odd, count, block)
        span = slice(step * nocc, (step + 1) * nocc)
        table[jnp.where(core == 0, near, across)] = packed[span]
        table[jnp.where(core == 0, across, near)] = swapped[span]
    table[origin_of(shared, count, block)] = last[...]
    for source, chosen in enumerate(chosen_by):
        for slot in range(slots):
            dens[source, :, slot * width : (slot + 1) * width] = table[chosen[slot]]
    flags = control[...].astype(jnp.float32)
    targeted = [jnp.max(flags[i : i + 1]) > 0.5 for i in range(2 * segs)]

    def halves(source, first, number):
        centre = (rows, rows_other.at[0, 0])[source]
        wide = centre[:, :, first * aux : (first + number) * aux].reshape(slots * width, number * aux)
        return jnp.dot(dens[source], wide, preferred_element_type=jnp.float32).astype(jnp.bfloat16)

    def lower_product(parts):
        total = jnp.zeros((nocc, nocc), jnp.float32)
        stack = jnp.concatenate(parts, 0)
        columns = [0.0] * (aux // BLOCK)
        for i in range(aux // BLOCK):
            lines = slice(i * BLOCK, (i + 1) * BLOCK)
            wide = jnp.dot(stack[:, lines], matrix[lines, i * BLOCK :], preferred_element_type=jnp.float32)
            for j in range(i, aux // BLOCK):
                piece = wide[:, (j - i) * BLOCK : (j - i + 1) * BLOCK]
                columns[j] += 0.5 * piece if i == j else piece
        for i, column in enumerate(columns):
            fitted = column.astype(jnp.bfloat16)
            for seg, part in enumerate(parts):
                total += lax.dot_general(
                    fitted[seg * nocc : (seg + 1) * nocc], part[:, i * BLOCK : (i + 1) * BLOCK], TRANSPOSED,
                    preferred_element_type=jnp.float32,
                )
        return total

    total_ref[...] = jnp.zeros_like(total_ref)
    for source in range(2):
        mine = targeted[source * segs : (source + 1) * segs]
        every = functools.reduce(jnp.logical_and, mine)

        @pl.when(every)
        def _():
            half = halves(source, 0, segs)
            total_ref[...] += lower_product([half[:, seg * aux : (seg + 1) * aux] for seg in range(segs)])

        for seg in range(segs):

            @pl.when(mine[seg] & ~every)
            def _():
                total_ref[...] += lower_product([halves(source, seg, 1)])

    out[0, 0] = total_ref[...] + total_ref[...].T


def local(count, density, three_centre, pattern, domain, owner, metric):
    nocc = density.shape[0]
    slots, width = three_centre.shape[2:4]
    segs = domain.shape[2]
    plan, shared = routes(count)
    received = [between_blocks(density, even, odd) for even, odd in plan]
    last = between_blocks(density, shared, shared)
    centre_other = swap_cores(three_centre)
    vmem = pl.BlockSpec(memory_space=pltpu.VMEM)
    hbm = pl.BlockSpec(memory_space=pltpu.HBM)
    limit = 24 * 1024 * 1024
    lines = -(-slots // 16) * 16
    own, rows, matrix, message, control = pl.pallas_call(
        stage_kernel,
        out_shape=(
            jax.ShapeDtypeStruct(density.shape, density.dtype),
            jax.ShapeDtypeStruct(three_centre.shape[2:], three_centre.dtype),
            jax.ShapeDtypeStruct(metric.shape[2:], metric.dtype),
            jax.ShapeDtypeStruct((lines, width), density.dtype),
            jax.ShapeDtypeStruct((-(-2 * segs // 8) * 8, 128), jnp.int32),
        ),
        in_specs=[hbm] * 6,
        out_specs=[vmem] * 5,
        scratch_shapes=[
            pltpu.SMEM(pattern.shape, jnp.int32),
            pltpu.SMEM(domain.shape, jnp.int32),
            pltpu.SMEM(owner.shape, jnp.int32),
            pltpu.SemaphoreType.DMA((6,)),
        ],
        compiler_params=pltpu.CompilerParams(vmem_limit_bytes=limit),
    )(*[far(array) for array in (density, three_centre, metric, pattern, domain, owner)])
    for k in range(len(received)):
        received[k], message = lax.optimization_barrier((received[k], message))
    last, _ = lax.optimization_barrier((last, message))
    last = pl.pallas_call(
        hold_kernel,
        out_shape=jax.ShapeDtypeStruct(last.shape, last.dtype),
        in_specs=[vmem],
        out_specs=vmem,
        compiler_params=pltpu.CompilerParams(vmem_limit_bytes=limit),
        cost_estimate=pl.CostEstimate(flops=1400000000, bytes_accessed=2 * last.size * 2, transcendentals=0),
    )(last)
    packed = jnp.concatenate(received + [message], 0)
    swapped = swap_cores(packed)
    return pl.pallas_call(
        functools.partial(exchange_kernel, plan, shared, count),
        out_shape=jax.ShapeDtypeStruct((1, 1, nocc, nocc), jnp.float32),
        in_specs=[vmem] * 9,
        out_specs=vmem,
        scratch_shapes=[
            pltpu.VMEM((count, nocc, width), jnp.bfloat16),
            pltpu.VMEM((2, nocc, slots * width), jnp.bfloat16),
            pltpu.VMEM((nocc, nocc), jnp.float32),
        ],
        compiler_params=pltpu.CompilerParams(vmem_limit_bytes=limit),
    )(own, last, packed, swapped, message, control, rows, centre_other, matrix)


def solution(mesh):
    in_specs = (
        P("groups", "blk"),
        P(("groups", "blk"), "atoms", None, None, None),
        P(("groups", "blk"), "atoms", None),
        P(("groups", "blk"), None, None),
        P(("groups", "blk"), None),
        P(("groups", "blk"), "atoms", None, None),
    )
    out_specs = P(("groups", "blk"), "atoms", None, None)
    body = functools.partial(local, mesh.shape["blk"])
    return jax.shard_map(body, mesh=mesh, in_specs=in_specs, out_specs=out_specs, check_vma=False)
```

```python
import functools
import jax
import jax.numpy as jnp
from jax import lax
from jax.experimental import pallas as pl
from jax.experimental.pallas import tpu as pltpu
from jax.sharding import PartitionSpec as P

AXES = ("blk", "atoms")
TRANSPOSED = (((1,), (1,)), ((), ()))
BLOCK = 256


def between_blocks(block, even, odd):
    pairs = []
    for targets, core in ((even, 0), (odd, 1)):
        pairs += [(2 * b + core, 2 * target + core) for b, target in enumerate(targets)]
    return lax.ppermute(block, AXES, pairs)


def swap_cores(block):
    return lax.ppermute(block, "atoms", [(0, 1), (1, 0)])


def far(array):
    return pltpu.with_memory_space_constraint(array, pltpu.HBM)


EIGHT = (
    ((1, 3, 4, 5, 2, 7, 0, 6), (6, 5, 1, 7, 0, 3, 2, 4), (7, 4, 0, 1, 6, 2, 5, 3), (2, 0, 3, 6, 7, 1, 4, 5)),
    ((3, 6, 7, 4, 5, 0, 1, 2), (4, 7, 5, 2, 1, 6, 3, 0), (5, 2, 6, 0, 3, 4, 7, 1), (2, 0, 3, 6, 7, 1, 4, 5)),
)


def routes(count):
    if count == 8:
        return list(zip(EIGHT[0][:3], EIGHT[1][:3])), EIGHT[0][3]
    shifts = [tuple((b + k) % count for b in range(count)) for k in range(count - 1, 1, -1)]
    shared = tuple((b + 1) % count for b in range(count))
    shifts += [shared] * (len(shifts) % 2)
    return list(zip(shifts[::2], shifts[1::2])), shared


def origin_of(targets, count, block):
    origin = jnp.int32(0)
    for b, target in enumerate(targets):
        origin = jnp.where(block == target, b, origin)
    return origin


def stage_kernel(*refs):
    (density, centre, metric), indices_far = refs[:3], refs[3:6]
    own, rows, matrix, message, control = refs[6:11]
    indices, sem = refs[11:14], refs[14]
    pattern, domain, owner = indices
    copies = [pltpu.make_async_copy(away, near, sem.at[i]) for i, (away, near) in enumerate(zip(indices_far, indices))]
    loads = [
        pltpu.make_async_copy(density, own, sem.at[3]),
        pltpu.make_async_copy(centre.at[0, 0], rows, sem.at[4]),
    ]
    aux = matrix.shape[0]
    for number, start in enumerate(range(0, aux, BLOCK)):
        lines, columns = pl.ds(start, BLOCK), pl.ds(start, aux - start)
        loads.append(
            pltpu.make_async_copy(metric.at[0, 0, lines, columns], matrix.at[lines, columns], sem.at[5 + number])
        )
    for copy in copies + loads:
        copy.start()
    for copy in copies:
        copy.wait()
    core = lax.axis_index("atoms")
    segs, slots = domain.shape[2], pattern.shape[2]
    line = lax.broadcasted_iota(jnp.int32, message.shape, 0)
    chosen = jnp.zeros(message.shape, jnp.int32)
    for slot in range(slots):
        chosen = jnp.where(line == slot, pattern[0, 0, slot], chosen)
    message[...] = chosen.astype(jnp.float32).astype(message.dtype)
    line = lax.broadcasted_iota(jnp.int32, control.shape, 0)
    mine = jnp.zeros(control.shape, jnp.int32)
    for source in range(2):
        origin = core if source == 0 else 1 - core
        for seg in range(segs):
            target = owner[0, domain[0, origin, seg]]
            mine = jnp.where(line == source * segs + seg, jnp.where(target == core, 1, 0), mine)
    control[...] = mine
    for load in loads:
        load.wait()


def hold_kernel(given, taken):
    taken[...] = given[...]


def exchange_kernel(plan, shared, count, own, last, packed, swapped, message, control, rows, rows_other, matrix, out, table, dens, total_ref):
    block = lax.axis_index("blk")
    core = lax.axis_index("atoms")
    slots, width = rows.shape[0], rows.shape[1]
    aux = matrix.shape[1]
    segs = rows.shape[2] // aux
    nocc = dens.shape[1]
    end = nocc * len(plan)

    def slot_numbers(lines):
        values = lines.astype(jnp.float32)
        return [jnp.max(values[slot : slot + 1]).astype(jnp.int32) for slot in range(slots)]

    chosen_by = [slot_numbers(message[...]), slot_numbers(swapped[end:])]
    table[block] = own[...]
    for step, (even, odd) in enumerate(plan):
        near, across = origin_of(even, count, block), origin_of(odd, count, block)
        span = slice(step * nocc, (step + 1) * nocc)
        table[jnp.where(core == 0, near, across)] = packed[span]
        table[jnp.where(core == 0, across, near)] = swapped[span]
    table[origin_of(shared, count, block)] = last[...]
    for source, chosen in enumerate(chosen_by):
        for slot in range(slots):
            dens[source, :, slot * width : (slot + 1) * width] = table[chosen[slot]]
    flags = control[...].astype(jnp.float32)
    targeted = [jnp.max(flags[i : i + 1]) > 0.5 for i in range(2 * segs)]

    def halves(source, first, number):
        centre = (rows, rows_other.at[0, 0])[source]
        wide = centre[:, :, first * aux : (first + number) * aux].reshape(slots * width, number * aux)
        return jnp.dot(dens[source], wide, preferred_element_type=jnp.float32).astype(jnp.bfloat16)

    def lower_product(parts):
        total = jnp.zeros((nocc, nocc), jnp.float32)
        stack = jnp.concatenate(parts, 0)
        columns = [0.0] * (aux // BLOCK)
        for i in range(aux // BLOCK):
            lines = slice(i * BLOCK, (i + 1) * BLOCK)
            wide = jnp.dot(stack[:, lines], matrix[lines, i * BLOCK :], preferred_element_type=jnp.float32)
            for j in range(i, aux // BLOCK):
                piece = wide[:, (j - i) * BLOCK : (j - i + 1) * BLOCK]
                columns[j] += 0.5 * piece if i == j else piece
        for i, column in enumerate(columns):
            fitted = column.astype(jnp.bfloat16)
            for seg, part in enumerate(parts):
                total += lax.dot_general(
                    fitted[seg * nocc : (seg + 1) * nocc], part[:, i * BLOCK : (i + 1) * BLOCK], TRANSPOSED,
                    preferred_element_type=jnp.float32,
                )
        return total

    total_ref[...] = jnp.zeros_like(total_ref)
    for source in range(2):
        mine = targeted[source * segs : (source + 1) * segs]
        every = functools.reduce(jnp.logical_and, mine)

        @pl.when(every)
        def _():
            half = halves(source, 0, segs)
            total_ref[...] += lower_product([half[:, seg * aux : (seg + 1) * aux] for seg in range(segs)])

        for seg in range(segs):

            @pl.when(mine[seg] & ~every)
            def _():
                total_ref[...] += lower_product([halves(source, seg, 1)])

    out[0, 0] = total_ref[...] + total_ref[...].T


def local(count, density, three_centre, pattern, domain, owner, metric):
    nocc = density.shape[0]
    slots, width = three_centre.shape[2:4]
    segs = domain.shape[2]
    plan, shared = routes(count)
    received = [between_blocks(density, even, odd) for even, odd in plan]
    last = between_blocks(density, shared, shared)
    centre_other = swap_cores(three_centre)
    vmem = pl.BlockSpec(memory_space=pltpu.VMEM)
    hbm = pl.BlockSpec(memory_space=pltpu.HBM)
    limit = 24 * 1024 * 1024
    lines = -(-slots // 16) * 16
    own, rows, matrix, message, control = pl.pallas_call(
        stage_kernel,
        out_shape=(
            jax.ShapeDtypeStruct(density.shape, density.dtype),
            jax.ShapeDtypeStruct(three_centre.shape[2:], three_centre.dtype),
            jax.ShapeDtypeStruct(metric.shape[2:], metric.dtype),
            jax.ShapeDtypeStruct((lines, width), density.dtype),
            jax.ShapeDtypeStruct((-(-2 * segs // 8) * 8, 128), jnp.int32),
        ),
        in_specs=[hbm] * 6,
        out_specs=[vmem] * 5,
        scratch_shapes=[
            pltpu.SMEM(pattern.shape, jnp.int32),
            pltpu.SMEM(domain.shape, jnp.int32),
            pltpu.SMEM(owner.shape, jnp.int32),
            pltpu.SemaphoreType.DMA((5 + metric.shape[2] // BLOCK,)),
        ],
        compiler_params=pltpu.CompilerParams(vmem_limit_bytes=limit),
    )(*[far(array) for array in (density, three_centre, metric, pattern, domain, owner)])
    for k in range(len(received)):
        received[k], message = lax.optimization_barrier((received[k], message))
    last, _ = lax.optimization_barrier((last, message))
    last = pl.pallas_call(
        hold_kernel,
        out_shape=jax.ShapeDtypeStruct(last.shape, last.dtype),
        in_specs=[vmem],
        out_specs=vmem,
        compiler_params=pltpu.CompilerParams(vmem_limit_bytes=limit),
        cost_estimate=pl.CostEstimate(flops=1400000000, bytes_accessed=2 * last.size * 2, transcendentals=0),
    )(last)
    packed = jnp.concatenate(received + [message], 0)
    swapped = swap_cores(packed)
    return pl.pallas_call(
        functools.partial(exchange_kernel, plan, shared, count),
        out_shape=jax.ShapeDtypeStruct((1, 1, nocc, nocc), jnp.float32),
        in_specs=[vmem] * 9,
        out_specs=vmem,
        scratch_shapes=[
            pltpu.VMEM((count, nocc, width), jnp.bfloat16),
            pltpu.VMEM((2, nocc, slots * width), jnp.bfloat16),
            pltpu.VMEM((nocc, nocc), jnp.float32),
        ],
        compiler_params=pltpu.CompilerParams(vmem_limit_bytes=limit),
    )(own, last, packed, swapped, message, control, rows, centre_other, matrix)


def solution(mesh):
    in_specs = (
        P("groups", "blk"),
        P(("groups", "blk"), "atoms", None, None, None),
        P(("groups", "blk"), "atoms", None),
        P(("groups", "blk"), None, None),
        P(("groups", "blk"), None),
        P(("groups", "blk"), "atoms", None, None),
    )
    out_specs = P(("groups", "blk"), "atoms", None, None)
    body = functools.partial(local, mesh.shape["blk"])
    return jax.shard_map(body, mesh=mesh, in_specs=in_specs, out_specs=out_specs, check_vma=False)
```
